512 devices in a mesh: img: 32 (over y, x_lo, core), seq: 16 (over x_hi, z).
Axes of the slice: x: 4 (x_hi: 2, x_lo: 2; x = x_hi * 2 + x_lo), y: 8, z: 8, core: 2. Of those that a mesh axis runs over, the one named last changes fastest.
Arguments:
- query_rows: bfloat16 [65536, 1536], P(('img', 'seq')), parts along dimension 0, may hold values from -16 to 16
- key_rows: bfloat16 [65536, 1536], P(('img', 'seq')), parts along dimension 0, may hold values from -16 to 16
- value_rows: bfloat16 [65536, 1536], P(('img', 'seq')), parts along dimension 0, may hold values from -6 to 6
- qk_gain: float32 [2, 128], replicated, may hold values from 0.6 to 5.6
- w_latent: bfloat16 [1536, 64], replicated, may hold values from -3 to 3
- conv_in_w: bfloat16 [3, 3, 16, 512], replicated, may hold values from -0.5 to 0.5
- conv_in_b: float32 [512], replicated, may hold values from -3 to 3
- conv_w: bfloat16 [3, 3, 512, 512], P(None, None, None, 'seq'), may hold values from -0.09375 to 0.09375
- conv_b: float32 [512], replicated, may hold values from -3 to 3
Outputs:
- feature_tiles: bfloat16 [512, 16, 32, 512], P(('img', 'seq')), parts along dimension 0
The draws below stay inside these ranges and needn't reach their ends.
There are 32 independent parts, one for each index of `img`. The reference program is written for one: setup_inputs(seed, part) draws one part's arguments, and reference() takes and returns one part's arrays. A program takes and returns all parts, laid end to end along the dimension named above; an argument that names none is the same for every part. Nothing has to cross between parts.
All inputs are finite; a program needn't handle non-finite values.
Results may differ from the reference program's by a relative error of at most 0.017.
The reference program's roundings to bfloat16 on the way count: a program that leaves them out, or rounds other values in their place, can miss the bound.
Values may be sent and summed in bfloat16 or wider, within the bound.
No kernel may reach another device: no remote copies, remote signals or barrier semaphores. Data moves between devices by JAX's collectives and lax.ppermute only.
A program may use at most 128 MiB of HBM per device.

```python
import math
import jax
import jax.numpy as jnp
import numpy as np
from jax import lax

HW = 12
HD = 128
LC = 16
C = 512
GW = 64
TOKENS = 2048
GH = 32
TR = 4
TC = 4
TH = 8
TW = 16
TILES = 16


def draw_query_rows(key, part):
    key = jax.random.fold_in(key, 101)
    drawn = jnp.clip(jax.random.normal(key, (TOKENS, HW, HD), jnp.float32), -4.0, 4.0)
    return drawn.reshape(TOKENS, HW * HD).astype(jnp.bfloat16)


def draw_key_rows(key, part):
    key = jax.random.fold_in(key, 102)
    drawn = jnp.clip(jax.random.normal(key, (TOKENS, HW, HD), jnp.float32), -4.0, 4.0)
    return drawn.reshape(TOKENS, HW * HD).astype(jnp.bfloat16)


def draw_qk_gain(key, part):
    key = jax.random.fold_in(key, 103)
    gain_rows = jax.random.uniform(key, (2, HD), jnp.float32, 0.6, 1.6)
    return gain_rows


def shard_levels(own_key, shape, pieces, least, largest):
    def one(dim, blocks):
        draws = jax.random.uniform(jax.random.fold_in(jax.random.fold_in(own_key, 6), dim), (blocks,), jnp.float32, least / len(pieces), largest / len(pieces))
        return jnp.repeat(jnp.exp(draws), shape[dim] // blocks).reshape((-1,) + (1,) * (len(shape) - dim - 1))

    factor_of = one(*pieces[0])
    for cut in pieces[1:]:
        factor_of = factor_of * one(*cut)
    return factor_of


def noise(key, extent, scale, limit, pieces=(), kind=jnp.bfloat16):
    entries = scale * jax.random.normal(key, extent, jnp.float32)
    if pieces:
        entries = entries * shard_levels(key, extent, pieces, -0.22, 0.18)
    return jnp.clip(entries, -limit, limit).astype(kind)


def setup_inputs(seed: int = 0, part: int = 0) -> dict:
    key_of = jax.random.split(jax.random.key(seed), 10)
    part_splits = jax.random.split(jax.random.fold_in(key_of[9], part), 10)
    return {
        "query_rows": draw_query_rows(jax.random.fold_in(jax.random.fold_in(key_of[9], part), 71), part),
        "key_rows": draw_key_rows(jax.random.fold_in(jax.random.fold_in(key_of[9], part), 71), part),
        "value_rows": noise(part_splits[2], (TOKENS, HW * HD), 1.0, 6.0, ((0, 16),)),
        "qk_gain": draw_qk_gain(jax.random.fold_in(key_of[9], 71), part),
        "w_latent": noise(key_of[4], (HW * HD, 4 * LC), 0.5, 3.0),
        "conv_in_w": noise(key_of[5], (3, 3, LC, C), (9 * LC) ** -0.5, 0.5),
        "conv_in_b": noise(key_of[6], (C,), 0.5, 3.0, (), jnp.float32),
        "conv_w": noise(key_of[7], (3, 3, C, C), (9 * C) ** -0.5, 0.09375, ((3, 16),)),
        "conv_b": noise(key_of[8], (C,), 0.5, 3.0, (), jnp.float32),
    }


THETA = 10000.0
EPS_NORM = 1e-06
LATENT_SCALE = 0.3611
LATENT_SHIFT = 0.1159

def rope_tables(row_ids, col_ids, head_dim):
    t_dims = head_dim // 8
    s_dims = (head_dim - t_dims) // 2
    dim_index = np.arange(head_dim)
    pair_index = dim_index // 2
    t_pairs = t_dims // 2
    s_pairs = s_dims // 2
    axis_id = np.where(pair_index < t_pairs, 0, np.where(pair_index < t_pairs + s_pairs, 1, 2))
    local_index = np.where(axis_id == 0, pair_index, np.where(axis_id == 1, pair_index - t_pairs, pair_index - t_pairs - s_pairs))
    axis_dims = np.where(axis_id == 0, t_dims, s_dims)
    frequency = jnp.asarray((THETA ** (-2.0 * local_index / axis_dims)).astype(np.float32))
    on_rows = jnp.asarray((axis_id == 1).astype(np.float32))
    on_cols = jnp.asarray((axis_id == 2).astype(np.float32))
    angles = (row_ids.astype(jnp.float32)[:, None] * on_rows + col_ids.astype(jnp.float32)[:, None] * on_cols) * frequency
    return (jnp.cos(angles), jnp.sin(angles))

def pair_turn(head_dim):
    dim_index = np.arange(head_dim)
    turn_table = np.zeros((head_dim, head_dim), np.float32)
    turn_table[dim_index[1::2], dim_index[0::2]] = -1.0
    turn_table[dim_index[0::2], dim_index[1::2]] = 1.0
    return jnp.asarray(turn_table)

def prepare(raw_rows, gain_row, cosine, sine_part, turn_table):
    head_dim = turn_table.shape[0]
    head_count = raw_rows.shape[1] // head_dim
    shaped = raw_rows.astype(jnp.float32).reshape(raw_rows.shape[0], head_count, head_dim)
    mean_sq = lax.optimization_barrier(jnp.mean(shaped * shaped, axis=2, keepdims=True))
    normed = shaped * lax.rsqrt(mean_sq + EPS_NORM) * gain_row
    turned = jnp.einsum('thd,de->the', normed, turn_table, precision=lax.Precision.HIGHEST)
    return (normed * cosine[:, None, :] + turned * sine_part[:, None, :]).astype(jnp.bfloat16)

def conv_three(padded, weight):
    height = padded.shape[0] - 2
    width_px = padded.shape[1] - 2
    summed = None
    for tap_row in range(3):
        for tap_col in range(3):
            window = padded[tap_row:tap_row + height, tap_col:tap_col + width_px].reshape(height * width_px, -1)
            contrib = jnp.dot(window, weight[tap_row, tap_col], preferred_element_type=jnp.float32)
            summed = contrib if summed is None else summed + contrib
    return summed.reshape(height, width_px, -1)

def reference(query_rows, key_rows, value_rows, qk_gain, w_latent, conv_in_w, conv_in_b, conv_w, conv_b):
    token_ids = jnp.arange(TOKENS, dtype=jnp.int32)
    cosine, sine_part = rope_tables(token_ids // GW, token_ids % GW, HD)
    turn_table = pair_turn(HD)
    queries = prepare(query_rows, qk_gain[0], cosine, sine_part, turn_table)
    keys_ready = prepare(key_rows, qk_gain[1], cosine, sine_part, turn_table)
    values = value_rows.reshape(TOKENS, HW, HD).astype(jnp.float32)
    keys_wide = keys_ready.astype(jnp.float32)
    block_rows = math.gcd(TOKENS, 512)
    score_scale = 1.0 / math.sqrt(HD)

    def attend(query_block):
        scores = jnp.einsum('qhd,khd->hqk', query_block.astype(jnp.float32), keys_wide) * score_scale
        highest = lax.optimization_barrier(jnp.max(scores, axis=2, keepdims=True))
        weights = jnp.exp(scores - highest)
        total_mass = lax.optimization_barrier(jnp.sum(weights, axis=2))
        rounded = lax.optimization_barrier(weights.astype(jnp.bfloat16))
        summed = jnp.einsum('hqk,khd->hqd', rounded.astype(jnp.float32), values)
        return (summed / total_mass[:, :, None]).astype(jnp.bfloat16)
    attended = lax.map(attend, queries.reshape(TOKENS // block_rows, block_rows, HW, HD))
    attended = attended.transpose(0, 2, 1, 3).reshape(TOKENS, HW * HD)
    latent = jnp.dot(attended, w_latent, preferred_element_type=jnp.float32).astype(jnp.bfloat16)
    unpacked = latent.reshape(GH, GW, LC, 2, 2).transpose(0, 3, 1, 4, 2).reshape(2 * GH, 2 * GW, LC)
    latent_z = (unpacked.astype(jnp.float32) / LATENT_SCALE + LATENT_SHIFT).astype(jnp.bfloat16)
    padded_z = jnp.pad(latent_z, ((1, 1), (1, 1), (0, 0)))
    hidden = jax.nn.silu(conv_three(padded_z, conv_in_w) + conv_in_b).astype(jnp.bfloat16)
    padded_hidden = jnp.pad(hidden, ((1, 1), (1, 1), (0, 0)))
    decoded = (conv_three(padded_hidden, conv_w) + conv_b).astype(jnp.bfloat16)
    tiled = decoded.reshape(TR, 2 * TH, TC, 2 * TW, C).transpose(0, 2, 1, 3, 4)
    return tiled.reshape(TILES, 2 * TH, 2 * TW, C)
```

```python
import math

import jax
import jax.numpy as jnp
import numpy as np
from jax import lax
from jax.experimental import pallas as pl
from jax.experimental.pallas import tpu as pltpu
from jax.sharding import PartitionSpec as P

GW = 64
THETA = 10000.0
EPS_NORM = 1e-06
LATENT_SCALE = 0.3611
LATENT_SHIFT = 0.1159
VMEM_LIMIT = 24 * 1024 * 1024
PREP_VMEM_LIMIT = 56 * 1024 * 1024

SLOTS = 16
PER_STEP = 3
STEP_SLOTS = 4
HALO_W = 18
HALO_H = 10
PIECE = 192
ROW_PITCH = 24
HEAD = 128
SHARE_SCALE = 16.0
GROUPS = 4
GROUP_START = (0, 5, 9, 13)
GROUP_ROWS = 80


def head_slot(head):
    return (head // PER_STEP) * STEP_SLOTS + head % PER_STEP


def rope_parts(grid_rows, grid_cols, head_dim):
    t_dims = head_dim // 8
    s_dims = (head_dim - t_dims) // 2
    pair = np.arange(head_dim) // 2
    t_pairs, s_pairs = t_dims // 2, s_dims // 2
    axis_id = np.where(pair < t_pairs, 0, np.where(pair < t_pairs + s_pairs, 1, 2))
    local = np.where(
        axis_id == 0, pair, np.where(axis_id == 1, pair - t_pairs, pair - t_pairs - s_pairs)
    )
    freq = (THETA ** (-2.0 * local / np.where(axis_id == 0, t_dims, s_dims))).astype(np.float32)
    row_angle = np.arange(grid_rows, dtype=np.float32)[:, None] * (freq * (axis_id == 1))
    col_angle = np.arange(grid_cols, dtype=np.float32)[:, None] * (freq * (axis_id == 2))
    tables = []
    for angle in (row_angle, col_angle):
        wide = angle.astype(np.float32).astype(np.float64)
        tables += [np.cos(wide).astype(np.float32), np.sin(wide).astype(np.float32)]
    return tables


def phase_selector(channels, i, j):
    shape = (256, 9 * channels)
    row = lax.broadcasted_iota(jnp.int32, shape, 0)
    col = lax.broadcasted_iota(jnp.int32, shape, 1)
    dr = 2 * (row >> 7) + ((row >> 1) & 1) + (i - 1)
    dc = 2 * ((row >> 6) & 1) + (row & 1) + (j - 1)
    target = (dr * 3 + dc) * channels + ((row & 63) >> 2)
    taken = (dr >= 0) & (dr < 3) & (dc >= 0) & (dc < 3) & (col == target)
    return jnp.where(taken, 1.0, 0.0).astype(jnp.bfloat16)


def prep_kernel(band_ref, q_ref, k_ref, v_ref, gain_ref, cr_ref, sr_ref, cc_ref, sc_ref, out_ref):
    tokens = q_ref.shape[0]
    band_rows = tokens // GW
    first = band_ref[0] * band_rows
    lane = lax.broadcasted_iota(jnp.int32, (GW, HEAD), 1)
    t_dims = HEAD // 8
    s_dims = (HEAD - t_dims) // 2
    on_cols = lane >= t_dims + s_dims
    cosine, sine = [], []
    for r in range(band_rows):
        cos_row = jnp.broadcast_to(cr_ref[pl.ds(first + r, 1), :], (GW, HEAD))
        sin_row = jnp.broadcast_to(sr_ref[pl.ds(first + r, 1), :], (GW, HEAD))
        cosine.append(jnp.where(on_cols, cc_ref[...], cos_row))
        sine.append(jnp.where(on_cols, sc_ref[...], sin_row))
    cosine = jnp.concatenate(cosine, axis=0)
    sine = jnp.concatenate(sine, axis=0)
    source = lax.broadcasted_iota(jnp.int32, (HEAD, HEAD), 0)
    target = lax.broadcasted_iota(jnp.int32, (HEAD, HEAD), 1)
    turn = jnp.where(
        (source ^ 1) == target, jnp.where((target & 1) == 0, -1.0, 1.0), 0.0
    ).astype(jnp.bfloat16)
    ones = jnp.full((HEAD, HEAD), 1.0, jnp.bfloat16)
    gains = gain_ref[...]
    even = lax.broadcasted_iota(jnp.int32, gains.shape, 1) % 2 == 0
    swapped = jnp.where(even, pltpu.roll(gains, HEAD - 1, 1), pltpu.roll(gains, 1, 1))

    def dot(x, y):
        return jnp.dot(x, y, preferred_element_type=jnp.float32)

    def ready(x, along, across):
        wide = x.astype(jnp.float32)
        squares = wide * wide
        high = squares.astype(jnp.bfloat16)
        low = (squares - high.astype(jnp.float32)).astype(jnp.bfloat16)
        mean = (dot(high, ones) + dot(low, ones)) * (1.0 / HEAD)
        turned = wide * along + dot(x, turn) * across
        return (turned * lax.rsqrt(mean + EPS_NORM)).astype(jnp.bfloat16)

    for which, ref in ((0, q_ref), (1, k_ref)):
        along = cosine * gains[which : which + 1, :]
        across = sine * swapped[which : which + 1, :]
        for h in range(PER_STEP):
            out_ref[h, which] = ready(ref[:, h * HEAD : (h + 1) * HEAD], along, across)
    for h in range(PER_STEP):
        out_ref[h, 2] = v_ref[:, h * HEAD : (h + 1) * HEAD]
    out_ref[PER_STEP] = jnp.zeros(out_ref.shape[1:], out_ref.dtype)


def prep(band, q, k, v, gain, tables):
    tokens = q.shape[0]
    wide = PER_STEP * HEAD
    rows = pl.BlockSpec((tokens, wide), lambda i, *_: (0, i))
    whole = lambda a: pl.BlockSpec(a.shape, lambda i, *_: (0, 0))
    return pl.pallas_call(
        prep_kernel,
        grid_spec=pltpu.PrefetchScalarGridSpec(
            num_scalar_prefetch=1,
            grid=(SLOTS // STEP_SLOTS,),
            in_specs=[rows, rows, rows, whole(gain)] + [whole(t) for t in tables],
            out_specs=pl.BlockSpec((STEP_SLOTS, 3, tokens, HEAD), lambda i, *_: (i, 0, 0, 0)),
        ),
        out_shape=jax.ShapeDtypeStruct((SLOTS, 3, tokens, HEAD), jnp.bfloat16),
        compiler_params=pltpu.CompilerParams(vmem_limit_bytes=PREP_VMEM_LIMIT),
        name="prep",
    )(band, q, k, v, gain, *tables)


def attend_kernel(place_ref, qkv_ref, wl_ref, out_ref, att_ref, cut_ref):
    sources, _, tok_dev, _ = qkv_ref.shape
    tokens = sources * tok_dev
    grid_rows = tokens // GW
    keys = qkv_ref[:, 1].reshape(tokens, HEAD)
    values = qkv_ref[:, 2].reshape(tokens, HEAD)
    factor = math.log2(math.e) / math.sqrt(HEAD)
    att_ref[0] = jnp.zeros(att_ref.shape[1:], jnp.float32)
    att_ref[grid_rows + 1] = jnp.zeros(att_ref.shape[1:], jnp.float32)
    edge = jnp.zeros((grid_rows + 2, 8, HEAD), jnp.float32)
    att_ref[:, 0:8, :] = edge
    att_ref[:, GW + 8 : GW + 16, :] = edge
    per_block = 2
    block = per_block * tok_dev
    block_rows = block // GW
    for b in range(sources // per_block):
        queries = qkv_ref[b * per_block : (b + 1) * per_block, 0].reshape(block, HEAD)
        scores = lax.dot_general(
            queries, keys, (((1,), (1,)), ((), ())), preferred_element_type=jnp.float32
        )
        highest = jnp.max(scores, axis=1, keepdims=True)
        weights = jnp.exp2((scores - highest) * factor)
        mass = jnp.sum(weights, axis=1, keepdims=True)
        summed = jnp.dot(weights.astype(jnp.bfloat16), values, preferred_element_type=jnp.float32)
        attended = (summed / mass).astype(jnp.bfloat16).astype(jnp.float32)
        att_ref[1 + b * block_rows : 1 + (b + 1) * block_rows, 8 : GW + 8, :] = attended.reshape(
            block_rows, GW, HEAD
        )
    side = math.isqrt(sources)
    for t in range(sources):
        top, left = (t // side) * (HALO_H - 2), (t % side) * (HALO_W - 2) + 7
        for r in range(HALO_H):
            cut_ref[t, r * HALO_W : (r + 1) * HALO_W, :] = att_ref[top + r, left : left + HALO_W, :]
        cut_ref[t, HALO_H * HALO_W : PIECE, :] = jnp.zeros(
            (PIECE - HALO_H * HALO_W, HEAD), jnp.float32
        )
    slot = place_ref[0]
    head = (slot // STEP_SLOTS) * PER_STEP + jnp.minimum(slot % STEP_SLOTS, PER_STEP - 1)
    weight = wl_ref[:, pl.ds(pl.multiple_of(head * HEAD, HEAD), HEAD)]
    empty = jnp.zeros_like(weight)
    weight = jnp.concatenate(
        [
            jnp.concatenate([weight, empty], axis=1),
            jnp.concatenate([empty, weight], axis=1),
        ],
        axis=0,
    )
    middle = PIECE // 2
    pairs = jnp.concatenate([cut_ref[:, :middle], cut_ref[:, middle:]], axis=2).astype(jnp.bfloat16)
    share = lax.dot_general(
        pairs.reshape(sources * middle, 2 * HEAD),
        weight,
        (((1,), (1,)), ((), ())),
        preferred_element_type=jnp.float32,
    )
    out_ref[...] = (share * SHARE_SCALE).reshape(out_ref.shape)


def attend(place, qkv, w_latent_t):
    sources, _, tok_dev, _ = qkv.shape
    tokens = sources * tok_dev
    return pl.pallas_call(
        attend_kernel,
        in_specs=[pl.BlockSpec(memory_space=pltpu.SMEM)] + [pl.BlockSpec(memory_space=pltpu.VMEM)] * 2,
        out_specs=pl.BlockSpec(memory_space=pltpu.VMEM),
        out_shape=jax.ShapeDtypeStruct((sources, PIECE // 2, 2 * w_latent_t.shape[0]), jnp.float32),
        scratch_shapes=[
            pltpu.VMEM((tokens // GW + 2, GW + 16, HEAD), jnp.float32),
            pltpu.VMEM((sources, PIECE, HEAD), jnp.float32),
        ],
        compiler_params=pltpu.CompilerParams(vmem_limit_bytes=VMEM_LIMIT),
        cost_estimate=pl.CostEstimate(
            flops=4 * tokens * tokens * HEAD,
            bytes_accessed=4 * tokens * HEAD * 2,
            transcendentals=tokens * tokens,
        ),
        name="attend",
    )(place, qkv, w_latent_t)


def tap_weight(ref, tap, channels):
    blocks = []
    for lane_block in range(2):
        halves = []
        for half in range(2):
            tile = 2 * tap + half
            group = max(g for g in range(GROUPS) if GROUP_START[g] <= tile)
            at = 16 * (tile - GROUP_START[group])
            halves.append(ref[lane_block * GROUPS + group, :, at : at + 16, :])
        blocks.append(jnp.concatenate(halves, axis=1).reshape(channels, 128))
    return jnp.concatenate(blocks, axis=1)


def hidden_kernel(
    heads, side, place_ref, part_ref, win_ref, bin_ref, x_ref, z_ref, flat_ref, hid_ref
):
    tile_row, tile_col = lax.div(place_ref[0], side), lax.rem(place_ref[0], side)
    grid_rows, grid_cols = side * (HALO_H - 2), side * (HALO_W - 2)
    top = tile_row * (HALO_H - 2) - 1
    left = tile_col * (HALO_W - 2) - 1

    latent = None
    for h in range(heads):
        share = part_ref[head_slot(h)]
        latent = share if latent is None else latent + share
    latent = (latent * (1.0 / SHARE_SCALE)).astype(jnp.bfloat16).astype(jnp.float32)
    z = (latent / LATENT_SCALE + LATENT_SHIFT).astype(jnp.bfloat16).astype(jnp.float32)
    crossed = pltpu.roll(z, 64, 1)
    first_half = lax.broadcasted_iota(jnp.int32, z.shape, 1) < 64
    z_ref[: PIECE // 2] = jnp.where(first_half, z, crossed)
    z_ref[PIECE // 2 :] = jnp.where(first_half, crossed, z)
    flat_ref[...] = jnp.zeros(flat_ref.shape, jnp.float32)
    col = left + lax.broadcasted_iota(jnp.int32, (HALO_W, 128), 0)
    for r in range(HALO_H):
        row = top + r
        inside = (col >= 0) & (col < grid_cols) & (row >= 0) & (row < grid_rows)
        start = ROW_PITCH * (r + 1) + 8
        flat_ref[start : start + HALO_W, :] = jnp.where(
            inside, z_ref[r * HALO_W : (r + 1) * HALO_W, :], 0.0
        )

    count = ROW_PITCH * HALO_H
    low = lax.broadcasted_iota(jnp.int32, (count, 128), 1) < 64
    out_col = left + lax.broadcasted_iota(jnp.int32, (ROW_PITCH, 128), 0)
    lane_blocks = hid_ref.shape[1]
    for i in range(2):
        for j in range(2):
            taps = []
            for a in (i - 1, i):
                at = 8 + ROW_PITCH * (1 + a) + (j - 1)
                taps.append(
                    jnp.where(low, flat_ref[at : at + count, :], flat_ref[at + 1 : at + 1 + count, :])
                )
            taps = jnp.concatenate(taps, axis=1).astype(jnp.bfloat16)
            weight = jnp.dot(
                phase_selector(win_ref.shape[0] // 9, i, j), win_ref[...], preferred_element_type=jnp.float32
            ).astype(jnp.bfloat16)
            pre = jnp.dot(taps, weight, preferred_element_type=jnp.float32) + bin_ref[...]
            hidden = (pre * (1.0 / (1.0 + jnp.exp(-pre)))).astype(jnp.bfloat16).astype(jnp.float32)
            for r in range(HALO_H):
                row = top + r
                inside = (out_col >= 0) & (out_col < grid_cols) & (row >= 0) & (row < grid_rows)
                for n in range(lane_blocks):
                    piece = hidden[r * ROW_PITCH : (r + 1) * ROW_PITCH, n * 128 : (n + 1) * 128]
                    hid_ref[2 * r + i, n, pl.ds(j, ROW_PITCH, stride=2), :] = jnp.where(
                        inside, piece, 0.0
                    )

    height, width = x_ref.shape[2] - 2, x_ref.shape[3]
    per_half = lane_blocks // 2
    for dc in range(3):
        for n in range(lane_blocks):
            x_ref[n // per_half, dc, :, :, (n % per_half) * 128 : (n % per_half + 1) * 128] = hid_ref[
                1 : height + 3, n, 1 + dc : 1 + dc + width, :
            ].astype(jnp.bfloat16)


def hidden_windows(place, part, w_in, b_in, heads, side):
    channels = w_in.shape[1]
    height, width = 2 * (HALO_H - 2), 2 * (HALO_W - 2)
    vmem = pl.BlockSpec(memory_space=pltpu.VMEM)
    return pl.pallas_call(
        lambda *refs: hidden_kernel(heads, side, *refs),
        in_specs=[pl.BlockSpec(memory_space=pltpu.SMEM)] + [vmem] * 3,
        out_specs=vmem,
        out_shape=jax.ShapeDtypeStruct((2, 3, height + 2, width, channels // 2), jnp.bfloat16),
        scratch_shapes=[
            pltpu.VMEM((PIECE, 128), jnp.float32),
            pltpu.VMEM((ROW_PITCH * (HALO_H + 2) + 16, 128), jnp.float32),
            pltpu.VMEM((2 * HALO_H, channels // 128, 2 * ROW_PITCH, 128), jnp.float32),
        ],
        compiler_params=pltpu.CompilerParams(vmem_limit_bytes=VMEM_LIMIT),
        cost_estimate=pl.CostEstimate(
            flops=8 * ROW_PITCH * HALO_H * 256 * channels,
            bytes_accessed=8 * height * width * channels,
            transcendentals=4 * ROW_PITCH * HALO_H * channels,
        ),
        name="hidden",
    )(place, part, w_in, b_in)


def decode_kernel(image_ref, x_ref, own_ref, other_ref, b_ref, out_ref):
    half = lax.rem(image_ref[0], 2)
    height, width = out_ref.shape[0], out_ref.shape[1]
    total = None
    depth = x_ref.shape[-1]
    channels = out_ref.shape[2]
    for dr in range(3):
        left_side, right_side = [], []
        for dc in range(3):
            for which, ref in ((half, own_ref), (1 - half, other_ref)):
                left_side.append(
                    x_ref[which, dc, dr : dr + height, :, :].reshape(height * width, depth)
                )
                right_side.append(tap_weight(ref, dr * 3 + dc, channels))
        part = lax.dot_general(
            jnp.concatenate(left_side, axis=1),
            jnp.concatenate(right_side, axis=1),
            (((1,), (1,)), ((), ())),
            preferred_element_type=jnp.float32,
        )
        total = part if total is None else total + part
    out_ref[...] = (total + b_ref[...]).astype(jnp.bfloat16).reshape(out_ref.shape)


def decode(image, windows, own, other, bias):
    channels = bias.shape[1]
    height, width = windows.shape[2] - 2, windows.shape[3]
    vmem = pl.BlockSpec(memory_space=pltpu.VMEM)
    return pl.pallas_call(
        decode_kernel,
        in_specs=[pl.BlockSpec(memory_space=pltpu.SMEM)] + [vmem] * 4,
        out_specs=vmem,
        out_shape=jax.ShapeDtypeStruct((height, width, channels), jnp.bfloat16),
        compiler_params=pltpu.CompilerParams(vmem_limit_bytes=VMEM_LIMIT),
        cost_estimate=pl.CostEstimate(
            flops=2 * height * width * 9 * channels * channels,
            bytes_accessed=2 * 9 * channels * channels,
            transcendentals=0,
        ),
        name="decode",
    )(image, windows, own, other, bias)


def on_device(
    query_rows, key_rows, value_rows, qk_gain, w_latent, conv_in_w, conv_in_b, conv_w, conv_b
):
    devices = lax.axis_size("seq")
    my_index = lax.axis_index("seq")
    my_image = lax.axis_index("img")
    tokens = devices * query_rows.shape[0]
    heads = query_rows.shape[1] // HEAD
    channels = conv_in_w.shape[3]
    own_channels = conv_w.shape[3]

    flipped = conv_w.reshape(9, channels, own_channels).transpose(0, 2, 1)
    flipped = flipped.reshape(9 * own_channels, channels)
    images = lax.axis_size("img")
    per_y = images // (2 * GROUPS)
    my_piece = my_image // per_y
    group = lax.rem(my_piece, GROUPS)
    start = 16 * (5 * group - jnp.maximum(group - 1, 0))
    lane = lax.rem(my_image, 2) * (channels // 2) + 128 * (my_piece // GROUPS)
    piece = lax.dynamic_slice(flipped, (start, lane), (GROUP_ROWS, 128))
    pieces = lax.all_to_all(
        jnp.broadcast_to(piece[None], (devices,) + piece.shape), "seq", 0, 0, tiled=True
    )

    tables = [jnp.asarray(t) for t in rope_parts(tokens // GW, GW, HEAD)]
    place = jnp.reshape(my_index, (1,)).astype(jnp.int32)
    image = jnp.reshape(my_image, (1,)).astype(jnp.int32)
    send = prep(place, query_rows, key_rows, value_rows, qk_gain, tables)
    qkv = lax.all_to_all(send, "seq", 0, 0, tiled=True)

    pieces, _ = lax.optimization_barrier((pieces, send))
    along_y = [[q + per_y * y for y in range(2 * GROUPS)] for q in range(per_y)]
    own = lax.all_gather(pieces, "img", axis=0, axis_index_groups=along_y)

    shares = attend(place, qkv, w_latent.T)
    part = lax.all_to_all(shares.astype(jnp.float16), "seq", 0, 0, tiled=True)
    part = part.astype(jnp.float32)

    windows = hidden_windows(
        place,
        part,
        conv_in_w.reshape(9 * conv_in_w.shape[2], channels),
        conv_in_b[None],
        heads,
        math.isqrt(devices),
    )
    own, _ = lax.optimization_barrier((own, shares))
    other = lax.ppermute(own, "img", [(i, i ^ 1) for i in range(images)])
    result = decode(image, windows, own, other, conv_b[None])
    return result[None]


def solution(mesh):
    placed = (
        P(("img", "seq"), None),
        P(("img", "seq"), None),
        P(("img", "seq"), None),
        P(),
        P(),
        P(),
        P(),
        P(None, None, None, "seq"),
        P(),
    )
    return jax.shard_map(
        on_device,
        mesh=mesh,
        in_specs=placed,
        out_specs=P(("img", "seq"), None, None, None),
        check_vma=False,
    )
```

```python
import math

import jax
import jax.numpy as jnp
import numpy as np
from jax import lax
from jax.experimental import pallas as pl
from jax.experimental.pallas import tpu as pltpu
from jax.sharding import PartitionSpec as P

GW = 64
THETA = 10000.0
EPS_NORM = 1e-06
LATENT_SCALE = 0.3611
LATENT_SHIFT = 0.1159
VMEM_LIMIT = 24 * 1024 * 1024
PREP_VMEM_LIMIT = 56 * 1024 * 1024

SLOTS = 16
PER_STEP = 3
STEP_SLOTS = 4
HALO_W = 18
HALO_H = 10
PIECE = 192
ROW_PITCH = 24
HEAD = 128
SHARE_SCALE = 16.0
GROUPS = 4
GROUP_START = (0, 5, 9, 13)
GROUP_ROWS = 80


def head_slot(head):
    return (head // PER_STEP) * STEP_SLOTS + head % PER_STEP


def rope_parts(grid_rows, grid_cols, head_dim):
    t_dims = head_dim // 8
    s_dims = (head_dim - t_dims) // 2
    pair = np.arange(head_dim) // 2
    t_pairs, s_pairs = t_dims // 2, s_dims // 2
    axis_id = np.where(pair < t_pairs, 0, np.where(pair < t_pairs + s_pairs, 1, 2))
    local = np.where(
        axis_id == 0, pair, np.where(axis_id == 1, pair - t_pairs, pair - t_pairs - s_pairs)
    )
    freq = (THETA ** (-2.0 * local / np.where(axis_id == 0, t_dims, s_dims))).astype(np.float32)
    row_angle = np.arange(grid_rows, dtype=np.float32)[:, None] * (freq * (axis_id == 1))
    col_angle = np.arange(grid_cols, dtype=np.float32)[:, None] * (freq * (axis_id == 2))
    tables = []
    for angle in (row_angle, col_angle):
        wide = angle.astype(np.float32).astype(np.float64)
        tables += [np.cos(wide).astype(np.float32), np.sin(wide).astype(np.float32)]
    return tables


def phase_selector(channels, i, j):
    shape = (256, 9 * channels)
    row = lax.broadcasted_iota(jnp.int32, shape, 0)
    col = lax.broadcasted_iota(jnp.int32, shape, 1)
    dr = 2 * (row >> 7) + ((row >> 1) & 1) + (i - 1)
    dc = 2 * ((row >> 6) & 1) + (row & 1) + (j - 1)
    target = (dr * 3 + dc) * channels + ((row & 63) >> 2)
    taken = (dr >= 0) & (dr < 3) & (dc >= 0) & (dc < 3) & (col == target)
    return jnp.where(taken, 1.0, 0.0).astype(jnp.bfloat16)


def prep_kernel(band_ref, q_ref, k_ref, v_ref, gain_ref, cr_ref, sr_ref, cc_ref, sc_ref, out_ref):
    tokens = q_ref.shape[0]
    band_rows = tokens // GW
    first = band_ref[0] * band_rows
    lane = lax.broadcasted_iota(jnp.int32, (GW, HEAD), 1)
    t_dims = HEAD // 8
    s_dims = (HEAD - t_dims) // 2
    on_cols = lane >= t_dims + s_dims
    cosine, sine = [], []
    for r in range(band_rows):
        cos_row = jnp.broadcast_to(cr_ref[pl.ds(first + r, 1), :], (GW, HEAD))
        sin_row = jnp.broadcast_to(sr_ref[pl.ds(first + r, 1), :], (GW, HEAD))
        cosine.append(jnp.where(on_cols, cc_ref[...], cos_row))
        sine.append(jnp.where(on_cols, sc_ref[...], sin_row))
    cosine = jnp.concatenate(cosine, axis=0)
    sine = jnp.concatenate(sine, axis=0)
    source = lax.broadcasted_iota(jnp.int32, (HEAD, HEAD), 0)
    target = lax.broadcasted_iota(jnp.int32, (HEAD, HEAD), 1)
    turn = jnp.where(
        (source ^ 1) == target, jnp.where((target & 1) == 0, -1.0, 1.0), 0.0
    ).astype(jnp.bfloat16)
    ones = jnp.full((HEAD, HEAD), 1.0, jnp.bfloat16)
    gains = gain_ref[...]
    even = lax.broadcasted_iota(jnp.int32, gains.shape, 1) % 2 == 0
    swapped = jnp.where(even, pltpu.roll(gains, HEAD - 1, 1), pltpu.roll(gains, 1, 1))

    def dot(x, y):
        return jnp.dot(x, y, preferred_element_type=jnp.float32)

    def ready(x, along, across):
        wide = x.astype(jnp.float32)
        squares = wide * wide
        high = squares.astype(jnp.bfloat16)
        low = (squares - high.astype(jnp.float32)).astype(jnp.bfloat16)
        mean = (dot(high, ones) + dot(low, ones)) * (1.0 / HEAD)
        turned = wide * along + dot(x, turn) * across
        return (turned * lax.rsqrt(mean + EPS_NORM)).astype(jnp.bfloat16)

    for which, ref in ((0, q_ref), (1, k_ref)):
        along = cosine * gains[which : which + 1, :]
        across = sine * swapped[which : which + 1, :]
        for h in range(PER_STEP):
            out_ref[h, which] = ready(ref[:, h * HEAD : (h + 1) * HEAD], along, across)
    for h in range(PER_STEP):
        out_ref[h, 2] = v_ref[:, h * HEAD : (h + 1) * HEAD]
    out_ref[PER_STEP] = jnp.zeros(out_ref.shape[1:], out_ref.dtype)


def prep(band, q, k, v, gain, tables):
    tokens = q.shape[0]
    wide = PER_STEP * HEAD
    rows = pl.BlockSpec((tokens, wide), lambda i, *_: (0, i))
    whole = lambda a: pl.BlockSpec(a.shape, lambda i, *_: (0, 0))
    return pl.pallas_call(
        prep_kernel,
        grid_spec=pltpu.PrefetchScalarGridSpec(
            num_scalar_prefetch=1,
            grid=(SLOTS // STEP_SLOTS,),
            in_specs=[rows, rows, rows, whole(gain)] + [whole(t) for t in tables],
            out_specs=pl.BlockSpec((STEP_SLOTS, 3, tokens, HEAD), lambda i, *_: (i, 0, 0, 0)),
        ),
        out_shape=jax.ShapeDtypeStruct((SLOTS, 3, tokens, HEAD), jnp.bfloat16),
        compiler_params=pltpu.CompilerParams(vmem_limit_bytes=PREP_VMEM_LIMIT),
        name="prep",
    )(band, q, k, v, gain, *tables)


def attend_kernel(place_ref, qkv_ref, wl_ref, out_ref, att_ref, cut_ref):
    sources, _, tok_dev, _ = qkv_ref.shape
    tokens = sources * tok_dev
    grid_rows = tokens // GW
    keys = qkv_ref[:, 1].reshape(tokens, HEAD)
    values = qkv_ref[:, 2].reshape(tokens, HEAD)
    factor = math.log2(math.e) / math.sqrt(HEAD)
    att_ref[0] = jnp.zeros(att_ref.shape[1:], jnp.float32)
    att_ref[grid_rows + 1] = jnp.zeros(att_ref.shape[1:], jnp.float32)
    edge = jnp.zeros((grid_rows + 2, 8, HEAD), jnp.float32)
    att_ref[:, 0:8, :] = edge
    att_ref[:, GW + 8 : GW + 16, :] = edge
    per_block = 2
    block = per_block * tok_dev
    block_rows = block // GW
    for b in range(sources // per_block):
        queries = qkv_ref[b * per_block : (b + 1) * per_block, 0].reshape(block, HEAD)
        scores = lax.dot_general(
            queries, keys, (((1,), (1,)), ((), ())), preferred_element_type=jnp.float32
        )
        highest = jnp.max(scores, axis=1, keepdims=True)
        weights = jnp.exp2((scores - highest) * factor)
        mass = jnp.sum(weights, axis=1, keepdims=True)
        summed = jnp.dot(weights.astype(jnp.bfloat16), values, preferred_element_type=jnp.float32)
        attended = (summed / mass).astype(jnp.bfloat16).astype(jnp.float32)
        att_ref[1 + b * block_rows : 1 + (b + 1) * block_rows, 8 : GW + 8, :] = attended.reshape(
            block_rows, GW, HEAD
        )
    side = math.isqrt(sources)
    for t in range(sources):
        top, left = (t // side) * (HALO_H - 2), (t % side) * (HALO_W - 2) + 7
        for r in range(HALO_H):
            cut_ref[t, r * HALO_W : (r + 1) * HALO_W, :] = att_ref[top + r, left : left + HALO_W, :]
        cut_ref[t, HALO_H * HALO_W : PIECE, :] = jnp.zeros(
            (PIECE - HALO_H * HALO_W, HEAD), jnp.float32
        )
    slot = place_ref[0]
    head = (slot // STEP_SLOTS) * PER_STEP + jnp.minimum(slot % STEP_SLOTS, PER_STEP - 1)
    weight = wl_ref[:, pl.ds(pl.multiple_of(head * HEAD, HEAD), HEAD)]
    empty = jnp.zeros_like(weight)
    weight = jnp.concatenate(
        [
            jnp.concatenate([weight, empty], axis=1),
            jnp.concatenate([empty, weight], axis=1),
        ],
        axis=0,
    )
    middle = PIECE // 2
    pairs = jnp.concatenate([cut_ref[:, :middle], cut_ref[:, middle:]], axis=2).astype(jnp.bfloat16)
    share = lax.dot_general(
        pairs.reshape(sources * middle, 2 * HEAD),
        weight,
        (((1,), (1,)), ((), ())),
        preferred_element_type=jnp.float32,
    )
    out_ref[...] = (share * SHARE_SCALE).reshape(out_ref.shape)


def attend(place, qkv, w_latent_t):
    sources, _, tok_dev, _ = qkv.shape
    tokens = sources * tok_dev
    return pl.pallas_call(
        attend_kernel,
        in_specs=[pl.BlockSpec(memory_space=pltpu.SMEM)] + [pl.BlockSpec(memory_space=pltpu.VMEM)] * 2,
        out_specs=pl.BlockSpec(memory_space=pltpu.VMEM),
        out_shape=jax.ShapeDtypeStruct((sources, PIECE // 2, 2 * w_latent_t.shape[0]), jnp.float32),
        scratch_shapes=[
            pltpu.VMEM((tokens // GW + 2, GW + 16, HEAD), jnp.float32),
            pltpu.VMEM((sources, PIECE, HEAD), jnp.float32),
        ],
        compiler_params=pltpu.CompilerParams(vmem_limit_bytes=VMEM_LIMIT),
        cost_estimate=pl.CostEstimate(
            flops=4 * tokens * tokens * HEAD,
            bytes_accessed=4 * tokens * HEAD * 2,
            transcendentals=tokens * tokens,
        ),
        name="attend",
    )(place, qkv, w_latent_t)


def tap_weight(ref, tap, channels, my_piece):
    blocks = []
    for lane_block in range(2):
        halves = []
        for half in range(2):
            tile = 2 * tap + half
            group = max(g for g in range(GROUPS) if GROUP_START[g] <= tile)
            at = 16 * (tile - GROUP_START[group])
            shift = (my_piece + 2 * GROUPS - (lane_block * GROUPS + group)) & (2 * GROUPS - 1)
            halves.append(ref[shift, :, at : at + 16, :])
        blocks.append(jnp.concatenate(halves, axis=1).reshape(channels, 128))
    return jnp.concatenate(blocks, axis=1)


def hidden_kernel(
    heads, side, place_ref, part_ref, win_ref, bin_ref, x_ref, z_ref, flat_ref, hid_ref
):
    tile_row, tile_col = lax.div(place_ref[0], side), lax.rem(place_ref[0], side)
    grid_rows, grid_cols = side * (HALO_H - 2), side * (HALO_W - 2)
    top = tile_row * (HALO_H - 2) - 1
    left = tile_col * (HALO_W - 2) - 1

    latent = None
    for h in range(heads):
        share = part_ref[head_slot(h)]
        latent = share if latent is None else latent + share
    latent = (latent * (1.0 / SHARE_SCALE)).astype(jnp.bfloat16).astype(jnp.float32)
    z = (latent / LATENT_SCALE + LATENT_SHIFT).astype(jnp.bfloat16).astype(jnp.float32)
    crossed = pltpu.roll(z, 64, 1)
    first_half = lax.broadcasted_iota(jnp.int32, z.shape, 1) < 64
    z_ref[: PIECE // 2] = jnp.where(first_half, z, crossed)
    z_ref[PIECE // 2 :] = jnp.where(first_half, crossed, z)
    flat_ref[...] = jnp.zeros(flat_ref.shape, jnp.float32)
    col = left + lax.broadcasted_iota(jnp.int32, (HALO_W, 128), 0)
    for r in range(HALO_H):
        row = top + r
        inside = (col >= 0) & (col < grid_cols) & (row >= 0) & (row < grid_rows)
        start = ROW_PITCH * (r + 1) + 8
        flat_ref[start : start + HALO_W, :] = jnp.where(
            inside, z_ref[r * HALO_W : (r + 1) * HALO_W, :], 0.0
        )

    count = ROW_PITCH * HALO_H
    low = lax.broadcasted_iota(jnp.int32, (count, 128), 1) < 64
    out_col = left + lax.broadcasted_iota(jnp.int32, (ROW_PITCH, 128), 0)
    lane_blocks = hid_ref.shape[1]
    for i in range(2):
        for j in range(2):
            taps = []
            for a in (i - 1, i):
                at = 8 + ROW_PITCH * (1 + a) + (j - 1)
                taps.append(
                    jnp.where(low, flat_ref[at : at + count, :], flat_ref[at + 1 : at + 1 + count, :])
                )
            taps = jnp.concatenate(taps, axis=1).astype(jnp.bfloat16)
            weight = jnp.dot(
                phase_selector(win_ref.shape[0] // 9, i, j), win_ref[...], preferred_element_type=jnp.float32
            ).astype(jnp.bfloat16)
            pre = jnp.dot(taps, weight, preferred_element_type=jnp.float32) + bin_ref[...]
            hidden = (pre * (1.0 / (1.0 + jnp.exp(-pre)))).astype(jnp.bfloat16).astype(jnp.float32)
            for r in range(HALO_H):
                row = top + r
                inside = (out_col >= 0) & (out_col < grid_cols) & (row >= 0) & (row < grid_rows)
                for n in range(lane_blocks):
                    piece = hidden[r * ROW_PITCH : (r + 1) * ROW_PITCH, n * 128 : (n + 1) * 128]
                    hid_ref[2 * r + i, n, pl.ds(j, ROW_PITCH, stride=2), :] = jnp.where(
                        inside, piece, 0.0
                    )

    height, width = x_ref.shape[2] - 2, x_ref.shape[3]
    per_half = lane_blocks // 2
    for dc in range(3):
        for n in range(lane_blocks):
            x_ref[n // per_half, dc, :, :, (n % per_half) * 128 : (n % per_half + 1) * 128] = hid_ref[
                1 : height + 3, n, 1 + dc : 1 + dc + width, :
            ].astype(jnp.bfloat16)


def hidden_windows(place, part, w_in, b_in, heads, side):
    channels = w_in.shape[1]
    height, width = 2 * (HALO_H - 2), 2 * (HALO_W - 2)
    vmem = pl.BlockSpec(memory_space=pltpu.VMEM)
    return pl.pallas_call(
        lambda *refs: hidden_kernel(heads, side, *refs),
        in_specs=[pl.BlockSpec(memory_space=pltpu.SMEM)] + [vmem] * 3,
        out_specs=vmem,
        out_shape=jax.ShapeDtypeStruct((2, 3, height + 2, width, channels // 2), jnp.bfloat16),
        scratch_shapes=[
            pltpu.VMEM((PIECE, 128), jnp.float32),
            pltpu.VMEM((ROW_PITCH * (HALO_H + 2) + 16, 128), jnp.float32),
            pltpu.VMEM((2 * HALO_H, channels // 128, 2 * ROW_PITCH, 128), jnp.float32),
        ],
        compiler_params=pltpu.CompilerParams(vmem_limit_bytes=VMEM_LIMIT),
        cost_estimate=pl.CostEstimate(
            flops=8 * ROW_PITCH * HALO_H * 256 * channels,
            bytes_accessed=8 * height * width * channels,
            transcendentals=4 * ROW_PITCH * HALO_H * channels,
        ),
        name="hidden",
    )(place, part, w_in, b_in)


def decode_kernel(per_y, image_ref, x_ref, own_ref, other_ref, b_ref, out_ref):
    half = lax.rem(image_ref[0], 2)
    my_piece = lax.div(image_ref[0], per_y)
    height, width = out_ref.shape[0], out_ref.shape[1]
    total = None
    depth = x_ref.shape[-1]
    channels = out_ref.shape[2]
    for dr in range(3):
        left_side, right_side = [], []
        for dc in range(3):
            for which, ref in ((half, own_ref), (1 - half, other_ref)):
                left_side.append(
                    x_ref[which, dc, dr : dr + height, :, :].reshape(height * width, depth)
                )
                right_side.append(tap_weight(ref, dr * 3 + dc, channels, my_piece))
        part = lax.dot_general(
            jnp.concatenate(left_side, axis=1),
            jnp.concatenate(right_side, axis=1),
            (((1,), (1,)), ((), ())),
            preferred_element_type=jnp.float32,
        )
        total = part if total is None else total + part
    out_ref[...] = (total + b_ref[...]).astype(jnp.bfloat16).reshape(out_ref.shape)


def decode(image, windows, own, other, bias, per_y):
    channels = bias.shape[1]
    height, width = windows.shape[2] - 2, windows.shape[3]
    vmem = pl.BlockSpec(memory_space=pltpu.VMEM)
    return pl.pallas_call(
        lambda *refs: decode_kernel(per_y, *refs),
        in_specs=[pl.BlockSpec(memory_space=pltpu.SMEM)] + [vmem] * 4,
        out_specs=vmem,
        out_shape=jax.ShapeDtypeStruct((height, width, channels), jnp.bfloat16),
        compiler_params=pltpu.CompilerParams(vmem_limit_bytes=VMEM_LIMIT),
        cost_estimate=pl.CostEstimate(
            flops=2 * height * width * 9 * channels * channels,
            bytes_accessed=2 * 9 * channels * channels,
            transcendentals=0,
        ),
        name="decode",
    )(image, windows, own, other, bias)


def on_device(
    query_rows, key_rows, value_rows, qk_gain, w_latent, conv_in_w, conv_in_b, conv_w, conv_b
):
    devices = lax.axis_size("seq")
    my_index = lax.axis_index("seq")
    my_image = lax.axis_index("img")
    tokens = devices * query_rows.shape[0]
    heads = query_rows.shape[1] // HEAD
    channels = conv_in_w.shape[3]
    own_channels = conv_w.shape[3]

    flipped = conv_w.reshape(9, channels, own_channels).transpose(0, 2, 1)
    flipped = flipped.reshape(9 * own_channels, channels)
    images = lax.axis_size("img")
    per_y = images // (2 * GROUPS)
    my_piece = my_image // per_y
    group = lax.rem(my_piece, GROUPS)
    start = 16 * (5 * group - jnp.maximum(group - 1, 0))
    lane = lax.rem(my_image, 2) * (channels // 2) + 128 * (my_piece // GROUPS)
    piece = lax.dynamic_slice(flipped, (start, lane), (GROUP_ROWS, 128))
    pieces = lax.all_to_all(
        jnp.broadcast_to(piece[None], (devices,) + piece.shape), "seq", 0, 0, tiled=True
    )

    tables = [jnp.asarray(t) for t in rope_parts(tokens // GW, GW, HEAD)]
    place = jnp.reshape(my_index, (1,)).astype(jnp.int32)
    image = jnp.reshape(my_image, (1,)).astype(jnp.int32)
    send = prep(place, query_rows, key_rows, value_rows, qk_gain, tables)
    pieces, send = lax.optimization_barrier((pieces, send))
    qkv = lax.all_to_all(send, "seq", 0, 0, tiled=True)

    gathered = {0: pieces}
    for k in (4, 3, 5, 2, 6, 1, 7):
        route = [(i, (i + per_y * k) % images) for i in range(images)]
        gathered[k] = lax.ppermute(pieces, "img", route)

    shares = attend(place, qkv, w_latent.T)
    far = (4, 3, 5, 2, 6)
    arrived, shares = lax.optimization_barrier(([gathered[k] for k in far], shares))
    gathered.update(zip(far, arrived))
    part = lax.all_to_all(shares.astype(jnp.float16), "seq", 0, 0, tiled=True)
    part = part.astype(jnp.float32)

    windows = hidden_windows(
        place,
        part,
        conv_in_w.reshape(9 * conv_in_w.shape[2], channels),
        conv_in_b[None],
        heads,
        math.isqrt(devices),
    )
    gathered, _ = lax.optimization_barrier((gathered, part))
    own = jnp.stack([gathered[k] for k in range(2 * GROUPS)])
    other = lax.ppermute(own, "img", [(i, i ^ 1) for i in range(images)])
    result = decode(image, windows, own, other, conv_b[None], per_y)
    return result[None]


def solution(mesh):
    placed = (
        P(("img", "seq"), None),
        P(("img", "seq"), None),
        P(("img", "seq"), None),
        P(),
        P(),
        P(),
        P(),
        P(None, None, None, "seq"),
        P(),
    )
    return jax.shard_map(
        on_device,
        mesh=mesh,
        in_specs=placed,
        out_specs=P(("img", "seq"), None, None, None),
        check_vma=False,
    )
```
